32 devices in a mesh: pool: 2 (over x), context: 8 (over z, y), tensor: 2 (over core).
Axes of the slice: x: 2, y: 2, z: 4, core: 2. Of those that a mesh axis runs over, the one named last changes fastest.
Arguments:
- cache: bfloat16 [2, 8, 16, 576], P('pool', 'context'), may hold values from -6 to 6
- hit_slots: int32 [2, 8], P('pool'), may hold values from 0 to 7, each once within a row
- prefix_blocks: int32 [2], P('pool'), may hold values from 2 to 8, as said below
- suffix_len: int32 [2], P('pool'), may hold values from 128 to 512, as said below
- suffix_latent: bfloat16 [2, 512, 576], P('pool', 'context')
- suffix_query: bfloat16 [2, 512, 64, 576], P('pool', 'context', 'tensor')
- decode_hidden: bfloat16 [2, 2, 7168], P('pool'), may hold values from -6 to 6
- kv_down: bfloat16 [7168, 576], P(('context', 'tensor')), may hold values from -0.0625 to 0.0625
- kv_gain: float32 [512], replicated, may hold values from 0.1 to 1.9
- decode_query: bfloat16 [2, 2, 64, 576], P('pool', None, 'tensor')
Outputs:
- suffix_context: bfloat16 [2, 512, 64, 512], P('pool', 'context', 'tensor')
- decode_context: bfloat16 [2, 2, 64, 512], P('pool', None, 'tensor')
- decode_latent: bfloat16 [2, 2, 576], P('pool')
The draws below stay inside these ranges and needn't reach their ends.
Inputs may be any that keep to these rules, and one draw needn't show every extreme that they name: `prefix_blocks`: some request has all of its group's 8 slots as hits. `suffix_len`: some request has all 512 suffix tokens valid.
All inputs are finite; a program needn't handle non-finite values.
Results may differ from the reference program's by a relative error of at most 0.03.
Values may be sent and summed in bfloat16 or wider, within the bound.
No kernel may reach another device: no remote copies, remote signals or barrier semaphores. Data moves between devices by JAX's collectives and lax.ppermute only.
A program may use at most 128 MiB of HBM per device.

```python
import math
import jax
import jax.numpy as jnp
from jax import lax

D = 7168
H = 64
LAT = 512
ROPE = 64
KVW = 576
BLK = 16
DEC = 2
SUFFIX = 512
SLOTS = 8
N_POOL = 2


def base_latent(key):
    return jax.random.normal(key, (N_POOL, SUFFIX, KVW), jnp.float32)


def draw_suffix_latent(key, part):
    base = base_latent(key)
    return base.astype(jnp.bfloat16)


def draw_suffix_query(key, part):
    key = jax.random.fold_in(key, 11)
    queries = jax.random.normal(key, (N_POOL, SUFFIX, H, KVW), jnp.float32)
    return queries.astype(jnp.bfloat16)


def draw_decode_query(key, part):
    key = jax.random.fold_in(key, 13)
    queries = jax.random.normal(key, (N_POOL, DEC, H, KVW), jnp.float32)
    return queries.astype(jnp.bfloat16)


def draw_prefix_blocks(key, part):
    key = jax.random.fold_in(key, 21)
    counts = jax.random.randint(key, (N_POOL,), max(1, SLOTS // 3), SLOTS + 1)
    chosen = jax.random.randint(jax.random.fold_in(key, 1), (), 0, N_POOL)
    return jnp.where(jnp.arange(N_POOL) == chosen, SLOTS, counts).astype(jnp.int32)


def draw_suffix_len(key, part):
    key = jax.random.fold_in(key, 23)
    counts = jax.random.randint(key, (N_POOL,), max(1, SUFFIX // 4), SUFFIX + 1)
    chosen = jax.random.randint(jax.random.fold_in(key, 1), (), 0, N_POOL)
    return jnp.where(jnp.arange(N_POOL) == chosen, SUFFIX, counts).astype(jnp.int32)


def steps_of(key, extent, cuts, low, high):
    def one(position, parts):
        heights = jax.random.uniform(jax.random.fold_in(jax.random.fold_in(key, 6), position), (parts,), jnp.float32, low / len(cuts), high / len(cuts))
        return jnp.repeat(jnp.exp(heights), extent[position] // parts).reshape((-1,) + (1,) * (len(extent) - position - 1))

    level = one(*cuts[0])
    for cut in cuts[1:]:
        level = level * one(*cut)
    return level


def scatter_about(stream_key, extent, deviation, limit, shards=(), kind=jnp.bfloat16):
    result = deviation * jax.random.normal(stream_key, extent, jnp.float32)
    if shards:
        result = result * steps_of(stream_key, extent, shards, -0.22, 0.18)
    return jnp.clip(result, -limit, limit).astype(kind)


def setup_inputs(seed: int = 0) -> dict:
    keys = jax.random.split(jax.random.key(seed), 11)
    cache = scatter_about(keys[0], (N_POOL, SLOTS, BLK, KVW), 1.0, 6.0, ((0, 2), (1, 8)))
    hit_slots = jax.vmap(lambda own: jax.random.permutation(own, SLOTS))(jax.random.split(keys[1], N_POOL)).reshape((N_POOL, SLOTS)).astype(jnp.int32)
    prefix_blocks = draw_prefix_blocks(jax.random.fold_in(keys[10], 71), 0)
    suffix_len = draw_suffix_len(jax.random.fold_in(keys[10], 71), 0)
    suffix_latent = draw_suffix_latent(jax.random.fold_in(keys[10], 71), 0)
    suffix_query = draw_suffix_query(jax.random.fold_in(keys[10], 71), 0)
    decode_hidden = scatter_about(keys[6], (N_POOL, DEC, D), 1.0, 6.0, ((0, 2),))
    kv_down = scatter_about(keys[7], (D, KVW), D ** -0.5, 0.0625, ((0, 16),))
    kv_gain = jnp.clip(1.0 + 0.18 * jax.random.normal(keys[8], (LAT,), jnp.float32), 0.1, 1.9)
    decode_query = draw_decode_query(jax.random.fold_in(keys[10], 71), 0)
    return {"cache": cache, "hit_slots": hit_slots, "prefix_blocks": prefix_blocks, "suffix_len": suffix_len, "suffix_latent": suffix_latent, "suffix_query": suffix_query, "decode_hidden": decode_hidden, "kv_down": kv_down, "kv_gain": kv_gain, "decode_query": decode_query}


SCALE = 192.0 ** (-0.5)
NEG = -1e+30

def attend_rows(queries, key_rows, allowed):
    scores = jnp.einsum('rhc,kc->rhk', queries.astype(jnp.float32), key_rows.astype(jnp.float32)) * SCALE
    scores = jnp.where(allowed[:, None, :], scores, NEG)
    top = lax.optimization_barrier(jnp.max(scores, axis=-1, keepdims=True))
    weights = jnp.where(allowed[:, None, :], jnp.exp(scores - top), 0.0).astype(jnp.bfloat16)
    denom = lax.optimization_barrier(jnp.sum(weights.astype(jnp.float32), axis=-1))
    accum = jnp.einsum('rhk,kc->rhc', weights.astype(jnp.float32), key_rows[:, :LAT].astype(jnp.float32))
    return (accum / denom[..., None]).astype(jnp.bfloat16)

def rotate_latent(raw, kv_gain, positions):
    latent = raw[:, :LAT]
    normed = latent * lax.rsqrt(lax.optimization_barrier(jnp.mean(latent * latent, axis=-1, keepdims=True)) + 1e-06) * kv_gain
    half = ROPE // 2
    freq = 10000.0 ** (-jnp.arange(half, dtype=jnp.float32) / half)
    angle = positions[:, None] * freq[None, :]
    first = raw[:, LAT:LAT + half]
    second = raw[:, LAT + half:]
    cosine = jnp.cos(angle)
    sine = jnp.sin(angle)
    rotated = jnp.concatenate([first * cosine - second * sine, second * cosine + first * sine], axis=-1)
    return jnp.concatenate([normed, rotated], axis=-1).astype(jnp.bfloat16)

def reference(cache, hit_slots, prefix_blocks, suffix_len, suffix_latent, suffix_query, decode_hidden, kv_down, kv_gain, decode_query):
    suffix_out = []
    decode_out = []
    latent_out = []
    slot_ids = jnp.arange(SLOTS, dtype=jnp.int32)
    token_ids = jnp.arange(SUFFIX, dtype=jnp.int32)
    dec_ids = jnp.arange(DEC, dtype=jnp.int32)
    qblock = math.gcd(SUFFIX, 64)
    for group in range(N_POOL):
        hits = hit_slots[group]
        slot_live = jnp.any((hits[:, None] == slot_ids[None, :]) & (slot_ids < prefix_blocks[group])[:, None], axis=0)
        cache_rows = cache[group].reshape(SLOTS * BLK, KVW)
        cache_keep = jnp.repeat(slot_live, BLK)
        key_rows = jnp.concatenate([cache_rows, suffix_latent[group]], axis=0)
        group_query = suffix_query[group]

        def one_block(index):
            queries = lax.dynamic_slice_in_dim(group_query, index * qblock, qblock, 0)
            rows = index * qblock + jnp.arange(qblock, dtype=jnp.int32)
            allowed = jnp.concatenate([jnp.broadcast_to(cache_keep[None, :], (qblock, SLOTS * BLK)), token_ids[None, :] <= rows[:, None]], axis=1)
            return attend_rows(queries, key_rows, allowed)
        blocks = lax.map(one_block, jnp.arange(SUFFIX // qblock, dtype=jnp.int32))
        suffix_out.append(blocks.reshape(SUFFIX, H, LAT))
        raw = jnp.dot(decode_hidden[group], kv_down, preferred_element_type=jnp.float32)
        positions = (prefix_blocks[group] * BLK + suffix_len[group] + dec_ids).astype(jnp.float32)
        fresh = rotate_latent(raw, kv_gain, positions)
        latent_out.append(fresh)
        all_rows = jnp.concatenate([key_rows, fresh], axis=0)
        allowed = jnp.concatenate([jnp.broadcast_to(cache_keep[None, :], (DEC, SLOTS * BLK)), jnp.broadcast_to((token_ids < suffix_len[group])[None, :], (DEC, SUFFIX)), dec_ids[None, :] <= dec_ids[:, None]], axis=1)
        decode_out.append(attend_rows(decode_query[group], all_rows, allowed))
    return (jnp.stack(suffix_out), jnp.stack(decode_out), jnp.stack(latent_out))
```

```python
import functools
import math

import jax
import jax.numpy as jnp
from jax import lax
from jax.experimental import pallas as pl
from jax.experimental.pallas import tpu as pltpu
from jax.sharding import PartitionSpec as P

SCALE = 192.0 ** (-0.5)
FACTOR = SCALE * 1.4426950408889634
NEG = -1e30
TILE = 16
LANES = 128
WIDE = 640
TAIL = 48
RADIX = 4
GROUPS = 16


def in_vmem(array):
    return pltpu.with_memory_space_constraint(array, pltpu.VMEM)


def in_hbm(array):
    return pltpu.with_memory_space_constraint(array, pltpu.HBM)


def dot(left, right):
    return jnp.dot(left, right, preferred_element_type=jnp.float32)


def score(keys, queries):
    return lax.dot_general(keys, queries, (((1,), (1,)), ((), ())), preferred_element_type=jnp.float32)


def pack_kernel(down_ref, hidden_ref, latent_ref, cache_ref, out_ref):
    core = lax.axis_index("tensor")
    down = down_ref[...]
    part, width = down.shape
    if hidden_ref.shape[1] == part:
        hidden = hidden_ref[...]
    else:
        pair = 2 * part
        start = pl.multiple_of(lax.axis_index("context") * pair, LANES)
        window = hidden_ref[:, pl.ds(start, pair)]
        hidden = jnp.where(core == 0, window[:, :part], window[:, part:])
    raw = dot(hidden, down)
    high = raw.astype(jnp.bfloat16).astype(jnp.float32)
    low = raw - high
    tok, cached = latent_ref.shape[1], cache_ref.shape[1]
    rows = tok + cached
    lat = width // LANES * LANES
    dec = raw.shape[0]
    for tile in range(2):
        at = pl.multiple_of(core * (lat // 2) + tile * LANES, LANES)
        out_ref[tile * rows : tile * rows + tok, :] = latent_ref[0, :, pl.ds(at, LANES)]
        out_ref[tile * rows + tok : (tile + 1) * rows, :] = cache_ref[0, :, pl.ds(at, LANES)]
    rope = jnp.concatenate(
        [latent_ref[0, :, lat:].astype(jnp.float32), cache_ref[0, :, lat:].astype(jnp.float32)], axis=0
    )
    left, right = split_rows(rows)
    rope = jnp.where(core == 0, rope[: rows // 2], rope[rows // 2 :])
    side = WIDE - width
    gap = jnp.zeros((left - right, side), jnp.float32)
    pieces = [jnp.concatenate([rope[:left], jnp.concatenate([rope[left:], gap], axis=0)], axis=1)]
    pieces += [piece[:, i : i + LANES] for piece in (high, low) for i in range(0, lat, LANES)]
    pieces.append(jnp.concatenate([high[:, lat:], low[:, lat:]], axis=1))
    used = sum(piece.shape[0] for piece in pieces)
    pieces.append(jnp.zeros((TAIL - used, LANES), jnp.float32))
    out_ref[2 * rows :, :] = jnp.concatenate(pieces, axis=0).astype(jnp.bfloat16)


def split_rows(rows):
    left = (rows // 4 + 7) // 8 * 8
    return left, rows // 2 - left


def stack_kernel(*refs):
    for i, ref in enumerate(refs[:-1]):
        refs[-1][i] = ref[...]


def fold(scores, values, state):
    top = jnp.max(scores, axis=0, keepdims=True)
    if state is not None:
        top = jnp.maximum(top, state[0])
    weights = jnp.exp2((scores - top) * FACTOR)
    whole = jnp.sum(weights, axis=0, keepdims=True)
    mixed = dot(values, weights.astype(jnp.bfloat16))
    if state is not None:
        fade = jnp.exp2((state[0] - top) * FACTOR)
        whole = whole + state[1] * fade
        mixed = mixed + state[2] * fade
    return top, whole, mixed


def ahead(order, begin, finish):
    started = begin(order[0])
    for block, following in zip(order, order[1:] + [None]):
        next_started = None if following is None else begin(following)
        finish(block, started)
        started = next_started


def read_state(mixed_ref, stat_ref, block, lanes, at=0):
    lanes = slice(at, at + lanes)
    return stat_ref[block, 0:1, lanes], stat_ref[block, 1:2, lanes], mixed_ref[block, :, lanes]


def write_state(mixed_ref, stat_ref, block, lanes, state):
    stat_ref[block, 0:1, :lanes] = state[0]
    stat_ref[block, 1:2, :lanes] = state[1]
    mixed_ref[block, :, :lanes] = state[2]


def table_kernel(shape, hits_ref, prefix_ref, length_ref, *refs):
    layout, tok, cached, block_rows = shape
    *table_refs, turn_ref = refs
    me = lax.axis_index("context")
    prefix = prefix_ref[0]
    length = length_ref[0]
    slots = cached // block_rows
    first = LANES - tok

    lane = lax.broadcasted_iota(jnp.int32, (tok, LANES), 1)
    bound = jnp.where(lane < first, length - 1, me * tok + lane - first)
    token = lax.broadcasted_iota(jnp.int32, (tok, LANES), 0)
    for keys, table_ref in zip(layout, table_refs):
        for i, key in enumerate(keys):
            source = me ^ key
            at = i * (tok + cached)
            allowed = token + source * tok <= bound
            table_ref[at : at + tok] = jnp.where(allowed, 0.0, NEG).astype(jnp.bfloat16)
            for slot in range(slots):
                live = jnp.int32(0)
                for b in range(hits_ref.shape[1]):
                    hit = jnp.logical_and(hits_ref[0, b] == source * slots + slot, b < prefix)
                    live = jnp.where(hit, 1, live)
                spot = at + tok + slot * block_rows
                mask = jnp.where(jnp.full((block_rows, LANES), live, jnp.int32) == 1, 0.0, NEG)
                table_ref[spot : spot + block_rows] = mask.astype(jnp.bfloat16)

    dec, rope = turn_ref.shape[1:]
    half = rope // 2
    step = lax.broadcasted_iota(jnp.int32, (dec, rope), 0)
    lane = lax.broadcasted_iota(jnp.int32, (dec, rope), 1)
    number = jnp.where(lane < half, lane, lane - half).astype(jnp.float32)
    position = (prefix * block_rows + length + step).astype(jnp.float32)
    angle = position * jnp.exp2(number * (-math.log2(10000.0) / half))
    turn_ref[0] = jnp.cos(angle)
    sine = jnp.sin(angle)
    turn_ref[1] = jnp.where(lane < half, -sine, sine)


def swap_halves(x):
    half = x.shape[1] // 2
    return jnp.concatenate([x[:, half:], x[:, :half]], axis=1)


def load_keys(keys_ref, pairs, table_ref, rows, side):
    core = lax.axis_index("tensor")
    left, right = split_rows(rows)
    in_key = lax.broadcasted_iota(jnp.int32, (rows, LANES), 1) < LANES - side
    at = 0
    for mine, theirs in pairs:
        halves = [jnp.where(core == 0, mine, theirs), jnp.where(core == 0, theirs, mine)]
        lane = 0
        tails = []
        for half in halves:
            for tile in range(2):
                keys_ref[at : at + rows, lane : lane + LANES] = half[tile * rows : (tile + 1) * rows]
                lane += LANES
            tail = half[2 * rows :].astype(jnp.float32)
            tails += [tail[:left], swap_halves(tail[:right])]
        rope = jnp.concatenate(tails, axis=0).astype(jnp.bfloat16)
        keys_ref[at : at + rows, lane:] = jnp.where(in_key, rope, table_ref[at : at + rows])
        at += rows


def middle_kernel(shape, marked_ref, decode_ref, table_ref, *refs):
    counts, rows, side, order, blocks, loaded = shape
    kinds = len(counts)
    if loaded:
        mixed_ref, stat_ref = refs[2:]
        keys, values = refs[0][...], refs[1][...]
        before = ()
    else:
        mixed_ref, stat_ref, keys_ref, values_ref = refs[-4:]
        own, other = refs[:kinds], refs[kinds : 2 * kinds]
        before = refs[2 * kinds : -4]
        pairs = [(mine[i], theirs[i]) for mine, theirs, n in zip(own, other, counts) for i in range(n)]
        load_keys(keys_ref, pairs, table_ref, rows, side)
        keys = keys_ref[...]
        values_ref[...] = keys_ref[:, : values_ref.shape[0]].T
        values = values_ref[...]
    lanes_all = mixed_ref.shape[2]

    def lanes_of(index):
        return LANES if order[index] == blocks - 1 else lanes_all

    def begin(index):
        if order[index] == blocks - 1:
            return score(keys, decode_ref[...]) + table_ref[...].astype(jnp.float32)
        return score(keys, marked_ref[index])

    def finish(index, scores):
        lanes = lanes_of(index)
        state = read_state(*before, index, lanes) if before else None
        write_state(mixed_ref, stat_ref, index, lanes, fold(scores, values, state))

    ahead(list(range(len(order))), begin, finish)


def last_kernel(
    shape, marked_ref, late_ref, decode_ref, table_ref, turn_ref, gain_ref, *refs
):
    counts, rows, heads, dec, width = shape
    kinds = len(counts)
    own, other = refs[:kinds], refs[kinds : 2 * kinds]
    states = [refs[2 * kinds : 2 * kinds + 2], refs[2 * kinds + 2 : 2 * kinds + 4]]
    out_hbm, decode_hbm, fresh_hbm = refs[2 * kinds + 4 : 2 * kinds + 7]
    keys_ref, out_ref, decode_out_ref, fresh_ref, sem = refs[2 * kinds + 7 :]
    cut, lat, lanes_all = states[0][0].shape
    blocks = cut + states[1][0].shape[0]
    steps = blocks - 1
    groups = lanes_all // heads
    side = WIDE - width

    def store(block, half):
        size = groups // 2
        return pltpu.make_async_copy(
            out_ref.at[block, pl.ds(half * size, size)],
            out_hbm.at[0, pl.ds(block * groups + half * size, size)],
            sem.at[block, half],
        )

    decode_store = pltpu.make_async_copy(decode_out_ref, decode_hbm, sem.at[steps, 0])
    fresh_store = pltpu.make_async_copy(fresh_ref, fresh_hbm, sem.at[steps, 1])

    pairs = [(own[-1][i], other[-1][i]) for i in range(counts[-1])]
    load_keys(keys_ref, pairs, table_ref, rows, side)
    values = keys_ref[:, :lat].T

    def fresh_keys():
        sums = None
        for ref, count in zip(own + other, counts + counts):
            for i in range(count):
                part = ref[i, 2 * rows :, :].astype(jnp.float32)
                sums = part if sums is None else sums + part
        at = split_rows(rows)[0]
        pieces = [sums[at + i * dec : at + (i + 1) * dec] for i in range(2 * lat // LANES + 1)]
        tiles = lat // LANES
        raw = [pieces[i] + pieces[tiles + i] for i in range(tiles)]
        rope = pieces[-1][:, :side] + pieces[-1][:, side:]
        latent = jnp.concatenate(raw, axis=1)
        mean = jnp.sum(latent * latent, axis=-1, keepdims=True) * (1.0 / lat)
        normed = latent * lax.rsqrt(mean + 1e-06) * gain_ref[...]
        rotated = rope * turn_ref[0] + swap_halves(rope) * turn_ref[1]
        fresh = jnp.concatenate([normed, rotated], axis=1)
        fresh_ref[0] = fresh.astype(jnp.bfloat16)
        fresh = jnp.concatenate([fresh, jnp.zeros((dec, side), jnp.float32)], axis=1)
        fresh = jnp.concatenate([fresh, jnp.zeros((TILE - dec, WIDE), jnp.float32)], axis=0)
        row = lax.broadcasted_iota(jnp.int32, (TILE, LANES), 0)
        lane = lax.broadcasted_iota(jnp.int32, (TILE, LANES), 1)
        shift = jnp.where(row <= lax.div(lane, heads), 0.0, NEG)
        return fresh.astype(jnp.bfloat16), jnp.where(row < dec, shift, NEG)

    fresh, fresh_shift = fresh_keys()
    fresh_store.start()

    def begin(block):
        if block == steps:
            return score(keys_ref[...], decode_ref[...]) + table_ref[...].astype(jnp.float32)
        return score(keys_ref[...], marked_ref[block] if block < cut else late_ref[block - cut])

    def finish(block, scores):
        half, index = (0, block) if block < cut else (1, block - cut)
        last = block == steps
        state = read_state(*states[half], index, LANES if last else lanes_all)
        state = fold(scores, values, state)
        if last:
            state = fold(score(fresh, decode_ref[...]) + fresh_shift, fresh[:, :lat].T, state)
        scale = 1.0 / state[1]
        if last:
            result = (state[2] * scale).astype(jnp.bfloat16).T
            decode_out_ref[0] = result[: dec * heads].reshape(dec, heads, lat)
            decode_store.start()
            return
        for half in range(2):
            some = slice(half * lanes_all // 2, (half + 1) * lanes_all // 2)
            result = (state[2][:, some] * scale[:, some]).astype(jnp.bfloat16).T
            out_ref[block, pl.ds(half * (groups // 2), groups // 2)] = result.reshape(-1, heads, lat)
            store(block, half).start()

    ahead([*range(steps - 1), steps, steps - 1], begin, finish)
    for block in range(steps):
        for half in range(2):
            store(block, half).wait()
    decode_store.wait()
    fresh_store.wait()


def on_device(
    cache,
    hit_slots,
    prefix_blocks,
    suffix_len,
    suffix_latent,
    suffix_query,
    decode_hidden,
    kv_down,
    kv_gain,
    decode_query,
    count,
):
    lat = kv_gain.shape[0]
    own_slots, block_rows, width = cache.shape[1:]
    cached = own_slots * block_rows
    tok = suffix_latent.shape[1]
    dec, heads = decode_query.shape[1:3]
    radix = math.gcd(count, RADIX)
    pages = count // radix
    vmem = pl.BlockSpec(memory_space=pltpu.VMEM)
    smem = pl.BlockSpec(memory_space=pltpu.SMEM)
    anywhere = pl.BlockSpec(memory_space=pl.ANY)
    small = pltpu.CompilerParams(vmem_limit_bytes=8 << 20)
    large = pltpu.CompilerParams(vmem_limit_bytes=24 << 20)

    part = kv_down.shape[0]
    hidden = decode_hidden[0]
    if 2 * part % LANES:
        part_index = lax.axis_index(("context", "tensor"))
        hidden = lax.dynamic_slice_in_dim(hidden, part_index * part, part, 1)
    block = tok + cached
    rows = 2 * block + TAIL
    message = pl.pallas_call(
        pack_kernel,
        out_shape=pltpu.VMEM((rows, LANES), jnp.bfloat16),
        in_specs=[vmem] * 4,
        out_specs=vmem,
        compiler_params=small,
    )(in_hbm(kv_down), in_hbm(hidden), in_hbm(suffix_latent), in_hbm(cache.reshape(1, cached, width)))

    def send(array, hop):
        return lax.ppermute(array, "context", [(rank, rank ^ hop) for rank in range(count)])

    def swap(array):
        return lax.ppermute(array, "tensor", [(0, 1), (1, 0)])

    def stack(*arrays):
        return pl.pallas_call(
            stack_kernel,
            out_shape=pltpu.VMEM((len(arrays), rows, LANES), jnp.bfloat16),
            in_specs=[vmem] * len(arrays),
            out_specs=vmem,
            compiler_params=small,
        )(*arrays)

    hops = list(range(1, pages))
    leaps = [digit * pages for digit in range(1, radix)]
    layout = [[0, *hops, *leaps]] + [[leap + hop for leap in leaps] for hop in hops]
    beside = [send(message, hop) for hop in hops]
    across = [send(message, leap) for leap in leaps]

    groups = math.gcd(tok, GROUPS)
    steps = tok // groups
    lanes = groups * heads
    blocks = steps + 1

    *tables, turn = pl.pallas_call(
        functools.partial(table_kernel, (layout, tok, cached, block_rows)),
        out_shape=tuple(pltpu.VMEM((len(keys) * block, LANES), jnp.bfloat16) for keys in layout)
        + (pltpu.VMEM((2, dec, width - lat), jnp.float32),),
        in_specs=[smem, smem, smem],
        out_specs=(vmem,) * (len(layout) + 1),
        compiler_params=small,
    )(in_hbm(hit_slots), prefix_blocks, suffix_len)

    def mark(query, begin, end):
        part = query[0, begin * groups : end * groups]
        shape = part.shape[:2] + (WIDE - width,)
        owner = lax.broadcasted_iota(jnp.int32, shape, 0) + begin * groups
        hot = (owner == lax.broadcasted_iota(jnp.int32, shape, 2)).astype(jnp.bfloat16)
        return jnp.concatenate([part, hot], axis=2).reshape(end - begin, lanes, WIDE)

    decode_rows = jnp.pad(
        decode_query.reshape(dec * heads, width), ((0, LANES - dec * heads), (0, WIDE - width))
    )

    held = lax.optimization_barrier((turn, *tables, *beside, *across))
    turn, tables, held = held[0], held[1 : 1 + pages], held[1 + pages :]
    beside, across = held[: pages - 1], held[pages - 1 :]
    far = stack(*across)
    ends = [send(far, hop) for hop in hops]
    own = [stack(message, *beside), far]
    other = [swap(array) for array in own]
    early, far = lax.optimization_barrier((suffix_query, far))
    marked = mark(early, 0, steps - 1)

    def middle(marked, table, own, other, order, *state, loaded=()):
        counts = [array.shape[0] for array in own]
        size = sum(counts) * block
        inputs = [in_vmem(marked), in_vmem(decode_rows), table, *(loaded or (*own, *other)), *state]
        aliases = {len(inputs) - 2: 0, len(inputs) - 1: 1} if state else {}
        kept = () if loaded else ((size, WIDE), (lat, size))
        return pl.pallas_call(
            functools.partial(
                middle_kernel, (counts, block, WIDE - width, order, blocks, bool(loaded))
            ),
            out_shape=(
                pltpu.VMEM((len(order), lat, lanes), jnp.float32),
                pltpu.VMEM((len(order), 8, lanes), jnp.float32),
                *(pltpu.VMEM(shape, jnp.bfloat16) for shape in kept),
            ),
            in_specs=[vmem] * len(inputs),
            out_specs=(vmem,) * (2 + len(kept)),
            input_output_aliases=aliases,
            compiler_params=large,
        )(*inputs)

    orders = list(range(blocks - 2)), [blocks - 2, blocks - 1]
    mixed, stat, *loaded = middle(marked, tables[0], own, other, orders[0])
    later, stat = lax.optimization_barrier((suffix_query, stat))
    late = mark(later, steps - 1, steps)
    mixed, stat, late, decode_rows, *ends = lax.optimization_barrier(
        (mixed, stat, late, decode_rows, *ends)
    )
    states = [
        (mixed, stat),
        middle(late, tables[0], own, other, orders[1], loaded=loaded)[:2],
    ]
    own += ends
    other += [swap(array) for array in ends]
    for number in range(1, pages - 1):
        chosen = slice(1 + number, 2 + number)
        states = [
            middle(part, tables[number], own[chosen], other[chosen], order, *state)[:2]
            for part, order, state in zip((marked, late), orders, states)
        ]
    counts = [array.shape[0] for array in own]
    return pl.pallas_call(
        functools.partial(last_kernel, (counts, block, heads, dec, width)),
        out_shape=(
            jax.ShapeDtypeStruct((1, tok, heads, lat), jnp.bfloat16),
            jax.ShapeDtypeStruct((1, dec, heads, lat), jnp.bfloat16),
            jax.ShapeDtypeStruct((1, dec, width), jnp.bfloat16),
        ),
        in_specs=[vmem] * (10 + 2 * len(own)),
        out_specs=(anywhere,) * 3,
        scratch_shapes=[
            pltpu.VMEM((counts[-1] * block, WIDE), jnp.bfloat16),
            pltpu.VMEM((steps, groups, heads, lat), jnp.bfloat16),
            pltpu.VMEM((1, dec, heads, lat), jnp.bfloat16),
            pltpu.VMEM((1, dec, width), jnp.bfloat16),
            pltpu.SemaphoreType.DMA((blocks, 2)),
        ],
        compiler_params=large,
    )(in_vmem(marked), in_vmem(late), in_vmem(decode_rows), tables[-1], turn, in_hbm(kv_gain.reshape(1, lat)), *own, *other, *states[0], *states[1])


def solution(mesh):
    placed = (
        P("pool", "context", None, None),
        P("pool", None),
        P("pool"),
        P("pool"),
        P("pool", "context", None),
        P("pool", "context", "tensor", None),
        P("pool", None, None),
        P(("context", "tensor"), None),
        P(),
        P("pool", None, "tensor", None),
    )
    return jax.shard_map(
        functools.partial(on_device, count=mesh.shape["context"]),
        mesh=mesh,
        in_specs=placed,
        out_specs=(
            P("pool", "context", "tensor", None),
            P("pool", None, "tensor", None),
            P("pool", None, None),
        ),
        check_vma=False,
    )
```

```python
import functools
import math

import jax
import jax.numpy as jnp
from jax import lax
from jax.experimental import pallas as pl
from jax.experimental.pallas import tpu as pltpu
from jax.sharding import PartitionSpec as P

SCALE = 192.0 ** (-0.5)
FACTOR = SCALE * 1.4426950408889634
NEG = -1e30
TILE = 16
LANES = 128
WIDE = 640
TAIL = 48
RADIX = 4
GROUPS = 16


def in_vmem(array):
    return pltpu.with_memory_space_constraint(array, pltpu.VMEM)


def in_hbm(array):
    return pltpu.with_memory_space_constraint(array, pltpu.HBM)


def dot(left, right):
    return jnp.dot(left, right, preferred_element_type=jnp.float32)


def score(keys, queries):
    return lax.dot_general(keys, queries, (((1,), (1,)), ((), ())), preferred_element_type=jnp.float32)


def pack_kernel(down_ref, hidden_ref, latent_ref, cache_ref, out_ref):
    core = lax.axis_index("tensor")
    down = down_ref[...]
    part, width = down.shape
    if hidden_ref.shape[1] == part:
        hidden = hidden_ref[...]
    else:
        pair = 2 * part
        start = pl.multiple_of(lax.axis_index("context") * pair, LANES)
        window = hidden_ref[:, pl.ds(start, pair)]
        hidden = jnp.where(core == 0, window[:, :part], window[:, part:])
    raw = dot(hidden, down)
    high = raw.astype(jnp.bfloat16).astype(jnp.float32)
    low = raw - high
    tok, cached = latent_ref.shape[1], cache_ref.shape[1]
    rows = tok + cached
    lat = width // LANES * LANES
    dec = raw.shape[0]
    for tile in range(2):
        at = pl.multiple_of(core * (lat // 2) + tile * LANES, LANES)
        out_ref[tile * rows : tile * rows + tok, :] = latent_ref[0, :, pl.ds(at, LANES)]
        out_ref[tile * rows + tok : (tile + 1) * rows, :] = cache_ref[0, :, pl.ds(at, LANES)]
    rope = jnp.concatenate(
        [latent_ref[0, :, lat:].astype(jnp.float32), cache_ref[0, :, lat:].astype(jnp.float32)], axis=0
    )
    left, right = split_rows(rows)
    rope = jnp.where(core == 0, rope[: rows // 2], rope[rows // 2 :])
    side = WIDE - width
    gap = jnp.zeros((left - right, side), jnp.float32)
    pieces = [jnp.concatenate([rope[:left], jnp.concatenate([rope[left:], gap], axis=0)], axis=1)]
    pieces += [piece[:, i : i + LANES] for piece in (high, low) for i in range(0, lat, LANES)]
    pieces.append(jnp.concatenate([high[:, lat:], low[:, lat:]], axis=1))
    used = sum(piece.shape[0] for piece in pieces)
    pieces.append(jnp.zeros((TAIL - used, LANES), jnp.float32))
    out_ref[2 * rows :, :] = jnp.concatenate(pieces, axis=0).astype(jnp.bfloat16)


def split_rows(rows):
    left = (rows // 4 + 7) // 8 * 8
    return left, rows // 2 - left


def stack_kernel(*refs):
    for i, ref in enumerate(refs[:-1]):
        refs[-1][i] = ref[...]


def fold(scores, values, state):
    top = jnp.max(scores, axis=0, keepdims=True)
    if state is not None:
        top = jnp.maximum(top, state[0])
    weights = jnp.exp2((scores - top) * FACTOR)
    whole = jnp.sum(weights, axis=0, keepdims=True)
    mixed = dot(values, weights.astype(jnp.bfloat16))
    if state is not None:
        fade = jnp.exp2((state[0] - top) * FACTOR)
        whole = whole + state[1] * fade
        mixed = mixed + state[2] * fade
    return top, whole, mixed


def ahead(order, begin, finish):
    started = begin(order[0])
    for block, following in zip(order, order[1:] + [None]):
        next_started = None if following is None else begin(following)
        finish(block, started)
        started = next_started


def read_state(mixed_ref, stat_ref, block, lanes, at=0):
    lanes = slice(at, at + lanes)
    return stat_ref[block, 0:1, lanes], stat_ref[block, 1:2, lanes], mixed_ref[block, :, lanes]


def write_state(mixed_ref, stat_ref, block, lanes, state):
    stat_ref[block, 0:1, :lanes] = state[0]
    stat_ref[block, 1:2, :lanes] = state[1]
    mixed_ref[block, :, :lanes] = state[2]


def table_kernel(shape, hits_ref, prefix_ref, length_ref, *refs):
    layout, tok, cached, block_rows = shape
    *table_refs, turn_ref, hot_ref = refs
    token = lax.broadcasted_iota(jnp.int32, hot_ref.shape, 0)
    hot = token == lax.broadcasted_iota(jnp.int32, hot_ref.shape, 2)
    hot_ref[...] = jnp.where(hot, 1.0, 0.0).astype(jnp.bfloat16)
    me = lax.axis_index("context")
    prefix = prefix_ref[0]
    length = length_ref[0]
    slots = cached // block_rows
    first = LANES - tok

    lane = lax.broadcasted_iota(jnp.int32, (tok, LANES), 1)
    bound = jnp.where(lane < first, length - 1, me * tok + lane - first)
    token = lax.broadcasted_iota(jnp.int32, (tok, LANES), 0)
    for keys, table_ref in zip(layout, table_refs):
        for i, key in enumerate(keys):
            source = me ^ key
            at = i * (tok + cached)
            allowed = token + source * tok <= bound
            table_ref[at : at + tok] = jnp.where(allowed, 0.0, NEG).astype(jnp.bfloat16)
            for slot in range(slots):
                live = jnp.int32(0)
                for b in range(hits_ref.shape[1]):
                    hit = jnp.logical_and(hits_ref[0, b] == source * slots + slot, b < prefix)
                    live = jnp.where(hit, 1, live)
                spot = at + tok + slot * block_rows
                mask = jnp.where(jnp.full((block_rows, LANES), live, jnp.int32) == 1, 0.0, NEG)
                table_ref[spot : spot + block_rows] = mask.astype(jnp.bfloat16)

    dec, rope = turn_ref.shape[1:]
    half = rope // 2
    step = lax.broadcasted_iota(jnp.int32, (dec, rope), 0)
    lane = lax.broadcasted_iota(jnp.int32, (dec, rope), 1)
    number = jnp.where(lane < half, lane, lane - half).astype(jnp.float32)
    position = (prefix * block_rows + length + step).astype(jnp.float32)
    angle = position * jnp.exp2(number * (-math.log2(10000.0) / half))
    turn_ref[0] = jnp.cos(angle)
    sine = jnp.sin(angle)
    turn_ref[1] = jnp.where(lane < half, -sine, sine)


def swap_halves(x):
    half = x.shape[1] // 2
    return jnp.concatenate([x[:, half:], x[:, :half]], axis=1)


def load_keys(keys_ref, pairs, table_ref, rows, side):
    core = lax.axis_index("tensor")
    left, right = split_rows(rows)
    in_key = lax.broadcasted_iota(jnp.int32, (rows, LANES), 1) < LANES - side
    at = 0
    for mine, theirs in pairs:
        halves = [jnp.where(core == 0, mine, theirs), jnp.where(core == 0, theirs, mine)]
        lane = 0
        tails = []
        for half in halves:
            for tile in range(2):
                keys_ref[at : at + rows, lane : lane + LANES] = half[tile * rows : (tile + 1) * rows]
                lane += LANES
            tail = half[2 * rows :].astype(jnp.float32)
            tails += [tail[:left], swap_halves(tail[:right])]
        rope = jnp.concatenate(tails, axis=0).astype(jnp.bfloat16)
        keys_ref[at : at + rows, lane:] = jnp.where(in_key, rope, table_ref[at : at + rows])
        at += rows


def middle_kernel(shape, marked_ref, decode_ref, table_ref, *refs):
    counts, rows, side, order, blocks, loaded = shape
    kinds = len(counts)
    if loaded:
        mixed_ref, stat_ref = refs[2:]
        keys, values = refs[0][...], refs[1][...]
        before = ()
    else:
        mixed_ref, stat_ref, keys_ref, values_ref = refs[-4:]
        own, other = refs[:kinds], refs[kinds : 2 * kinds]
        before = refs[2 * kinds : -4]
        pairs = [(mine[i], theirs[i]) for mine, theirs, n in zip(own, other, counts) for i in range(n)]
        load_keys(keys_ref, pairs, table_ref, rows, side)
        keys = keys_ref[...]
        values_ref[...] = keys_ref[:, : values_ref.shape[0]].T
        values = values_ref[...]
    lanes_all = mixed_ref.shape[2]

    def lanes_of(index):
        return LANES if order[index] == blocks - 1 else lanes_all

    def begin(index):
        if order[index] == blocks - 1:
            return score(keys, decode_ref[...]) + table_ref[...].astype(jnp.float32)
        return score(keys, marked_ref[index])

    def finish(index, scores):
        lanes = lanes_of(index)
        state = read_state(*before, index, lanes) if before else None
        write_state(mixed_ref, stat_ref, index, lanes, fold(scores, values, state))

    ahead(list(range(len(order))), begin, finish)


def last_kernel(
    shape, marked_ref, late_ref, decode_ref, table_ref, turn_ref, gain_ref, *refs
):
    counts, rows, heads, dec, width = shape
    kinds = len(counts)
    own, other = refs[:kinds], refs[kinds : 2 * kinds]
    states = [refs[2 * kinds : 2 * kinds + 2], refs[2 * kinds + 2 : 2 * kinds + 4]]
    out_hbm, decode_hbm, fresh_hbm = refs[2 * kinds + 4 : 2 * kinds + 7]
    keys_ref, out_ref, decode_out_ref, fresh_ref, sem = refs[2 * kinds + 7 :]
    cut, lat, lanes_all = states[0][0].shape
    blocks = cut + states[1][0].shape[0]
    steps = blocks - 1
    groups = lanes_all // heads
    side = WIDE - width

    def store(block, half):
        size = groups // 2
        return pltpu.make_async_copy(
            out_ref.at[block, pl.ds(half * size, size)],
            out_hbm.at[0, pl.ds(block * groups + half * size, size)],
            sem.at[block, half],
        )

    decode_store = pltpu.make_async_copy(decode_out_ref, decode_hbm, sem.at[steps, 0])
    fresh_store = pltpu.make_async_copy(fresh_ref, fresh_hbm, sem.at[steps, 1])

    pairs = [(own[-1][i], other[-1][i]) for i in range(counts[-1])]
    load_keys(keys_ref, pairs, table_ref, rows, side)
    values = keys_ref[:, :lat].T

    def fresh_keys():
        sums = None
        for ref, count in zip(own + other, counts + counts):
            for i in range(count):
                part = ref[i, 2 * rows :, :].astype(jnp.float32)
                sums = part if sums is None else sums + part
        at = split_rows(rows)[0]
        pieces = [sums[at + i * dec : at + (i + 1) * dec] for i in range(2 * lat // LANES + 1)]
        tiles = lat // LANES
        raw = [pieces[i] + pieces[tiles + i] for i in range(tiles)]
        rope = pieces[-1][:, :side] + pieces[-1][:, side:]
        latent = jnp.concatenate(raw, axis=1)
        mean = jnp.sum(latent * latent, axis=-1, keepdims=True) * (1.0 / lat)
        normed = latent * lax.rsqrt(mean + 1e-06) * gain_ref[...]
        rotated = rope * turn_ref[0] + swap_halves(rope) * turn_ref[1]
        fresh = jnp.concatenate([normed, rotated], axis=1)
        fresh_ref[0] = fresh.astype(jnp.bfloat16)
        fresh = jnp.concatenate([fresh, jnp.zeros((dec, side), jnp.float32)], axis=1)
        fresh = jnp.concatenate([fresh, jnp.zeros((TILE - dec, WIDE), jnp.float32)], axis=0)
        row = lax.broadcasted_iota(jnp.int32, (TILE, LANES), 0)
        lane = lax.broadcasted_iota(jnp.int32, (TILE, LANES), 1)
        shift = jnp.where(row <= lax.div(lane, heads), 0.0, NEG)
        return fresh.astype(jnp.bfloat16), jnp.where(row < dec, shift, NEG)

    fresh, fresh_shift = fresh_keys()
    fresh_store.start()

    def begin(block):
        if block == steps:
            return score(keys_ref[...], decode_ref[...]) + table_ref[...].astype(jnp.float32)
        return score(keys_ref[...], marked_ref[block] if block < cut else late_ref[block - cut])

    def finish(block, scores):
        half, index = (0, block) if block < cut else (1, block - cut)
        last = block == steps
        state = read_state(*states[half], index, LANES if last else lanes_all)
        state = fold(scores, values, state)
        if last:
            state = fold(score(fresh, decode_ref[...]) + fresh_shift, fresh[:, :lat].T, state)
        scale = 1.0 / state[1]
        if last:
            result = (state[2] * scale).astype(jnp.bfloat16).T
            decode_out_ref[0] = result[: dec * heads].reshape(dec, heads, lat)
            decode_store.start()
            return
        for half in range(2):
            some = slice(half * lanes_all // 2, (half + 1) * lanes_all // 2)
            result = (state[2][:, some] * scale[:, some]).astype(jnp.bfloat16).T
            out_ref[block, pl.ds(half * (groups // 2), groups // 2)] = result.reshape(-1, heads, lat)
            store(block, half).start()

    ahead([*range(steps - 1), steps, steps - 1], begin, finish)
    for block in range(steps):
        for half in range(2):
            store(block, half).wait()
    decode_store.wait()
    fresh_store.wait()


def on_device(
    cache,
    hit_slots,
    prefix_blocks,
    suffix_len,
    suffix_latent,
    suffix_query,
    decode_hidden,
    kv_down,
    kv_gain,
    decode_query,
    count,
):
    lat = kv_gain.shape[0]
    own_slots, block_rows, width = cache.shape[1:]
    cached = own_slots * block_rows
    tok = suffix_latent.shape[1]
    dec, heads = decode_query.shape[1:3]
    radix = math.gcd(count, RADIX)
    pages = count // radix
    vmem = pl.BlockSpec(memory_space=pltpu.VMEM)
    smem = pl.BlockSpec(memory_space=pltpu.SMEM)
    anywhere = pl.BlockSpec(memory_space=pl.ANY)
    small = pltpu.CompilerParams(vmem_limit_bytes=8 << 20)
    large = pltpu.CompilerParams(vmem_limit_bytes=24 << 20)

    part = kv_down.shape[0]
    hidden = decode_hidden[0]
    if 2 * part % LANES:
        part_index = lax.axis_index(("context", "tensor"))
        hidden = lax.dynamic_slice_in_dim(hidden, part_index * part, part, 1)
    block = tok + cached
    rows = 2 * block + TAIL
    message = pl.pallas_call(
        pack_kernel,
        out_shape=pltpu.VMEM((rows, LANES), jnp.bfloat16),
        in_specs=[vmem] * 4,
        out_specs=vmem,
        compiler_params=small,
    )(in_hbm(kv_down), in_hbm(hidden), in_hbm(suffix_latent), in_hbm(cache.reshape(1, cached, width)))

    def send(array, hop):
        return lax.ppermute(array, "context", [(rank, rank ^ hop) for rank in range(count)])

    def swap(array):
        return lax.ppermute(array, "tensor", [(0, 1), (1, 0)])

    def stack(*arrays):
        return pl.pallas_call(
            stack_kernel,
            out_shape=pltpu.VMEM((len(arrays), rows, LANES), jnp.bfloat16),
            in_specs=[vmem] * len(arrays),
            out_specs=vmem,
            compiler_params=small,
        )(*arrays)

    hops = list(range(1, pages))
    leaps = [digit * pages for digit in range(1, radix)]
    layout = [[0, *hops, *leaps]] + [[leap + hop for leap in leaps] for hop in hops]
    beside = [send(message, hop) for hop in hops]
    across = [send(message, leap) for leap in leaps]

    groups = math.gcd(tok, GROUPS)
    steps = tok // groups
    lanes = groups * heads
    blocks = steps + 1

    *tables, turn, hot = pl.pallas_call(
        functools.partial(table_kernel, (layout, tok, cached, block_rows)),
        out_shape=tuple(pltpu.VMEM((len(keys) * block, LANES), jnp.bfloat16) for keys in layout)
        + (
            pltpu.VMEM((2, dec, width - lat), jnp.float32),
            pltpu.VMEM((tok, heads, WIDE - width), jnp.bfloat16),
        ),
        in_specs=[smem, smem, smem],
        out_specs=(vmem,) * (len(layout) + 2),
        compiler_params=small,
    )(in_hbm(hit_slots), prefix_blocks, suffix_len)

    def mark(query, begin, end):
        some = slice(begin * groups, end * groups)
        return jnp.concatenate([query[0, some], hot[some]], axis=2).reshape(end - begin, lanes, WIDE)

    marked = mark(suffix_query, 0, steps - 1)
    held = lax.optimization_barrier((turn, hot, marked, *tables, *beside, *across))
    turn, hot, marked = held[:3]
    tables, held = held[3 : 3 + pages], held[3 + pages :]
    beside, across = held[: pages - 1], held[pages - 1 :]
    far = stack(*across)
    ends = [send(far, hop) for hop in hops]
    own = [stack(message, *beside), far]
    other = [swap(array) for array in own]

    def middle(marked, decode_rows, table, own, other, order, *state, loaded=()):
        counts = [array.shape[0] for array in own]
        size = sum(counts) * block
        decode_rows = hot if decode_rows is None else decode_rows
        inputs = [in_vmem(marked), in_vmem(decode_rows), table, *(loaded or (*own, *other)), *state]
        aliases = {len(inputs) - 2: 0, len(inputs) - 1: 1} if state else {}
        kept = () if loaded else ((size, WIDE), (lat, size))
        return pl.pallas_call(
            functools.partial(
                middle_kernel, (counts, block, WIDE - width, order, blocks, bool(loaded))
            ),
            out_shape=(
                pltpu.VMEM((len(order), lat, lanes), jnp.float32),
                pltpu.VMEM((len(order), 8, lanes), jnp.float32),
                *(pltpu.VMEM(shape, jnp.bfloat16) for shape in kept),
            ),
            in_specs=[vmem] * len(inputs),
            out_specs=(vmem,) * (2 + len(kept)),
            input_output_aliases=aliases,
            compiler_params=large,
        )(*inputs)

    orders = list(range(blocks - 2)), [blocks - 2, blocks - 1]
    mixed, stat, *loaded = middle(marked, None, tables[0], own, other, orders[0])
    later, decode_rows, stat = lax.optimization_barrier((suffix_query, decode_query, stat))
    late = mark(later, steps - 1, steps)
    decode_rows = jnp.pad(
        decode_rows.reshape(dec * heads, width), ((0, LANES - dec * heads), (0, WIDE - width))
    )
    mixed, stat, late, decode_rows, *ends = lax.optimization_barrier(
        (mixed, stat, late, decode_rows, *ends)
    )
    states = [
        (mixed, stat),
        middle(late, decode_rows, tables[0], own, other, orders[1], loaded=loaded)[:2],
    ]
    own += ends
    other += [swap(array) for array in ends]
    for number in range(1, pages - 1):
        chosen = slice(1 + number, 2 + number)
        states = [
            middle(part, decode_rows, tables[number], own[chosen], other[chosen], order, *state)[:2]
            for part, order, state in zip((marked, late), orders, states)
        ]
    counts = [array.shape[0] for array in own]
    return pl.pallas_call(
        functools.partial(last_kernel, (counts, block, heads, dec, width)),
        out_shape=(
            jax.ShapeDtypeStruct((1, tok, heads, lat), jnp.bfloat16),
            jax.ShapeDtypeStruct((1, dec, heads, lat), jnp.bfloat16),
            jax.ShapeDtypeStruct((1, dec, width), jnp.bfloat16),
        ),
        in_specs=[vmem] * (10 + 2 * len(own)),
        out_specs=(anywhere,) * 3,
        scratch_shapes=[
            pltpu.VMEM((counts[-1] * block, WIDE), jnp.bfloat16),
            pltpu.VMEM((steps, groups, heads, lat), jnp.bfloat16),
            pltpu.VMEM((1, dec, heads, lat), jnp.bfloat16),
            pltpu.VMEM((1, dec, width), jnp.bfloat16),
            pltpu.SemaphoreType.DMA((blocks, 2)),
        ],
        compiler_params=large,
    )(in_vmem(marked), in_vmem(late), in_vmem(decode_rows), tables[-1], turn, in_hbm(kv_gain.reshape(1, lat)), *own, *other, *states[0], *states[1])


def solution(mesh):
    placed = (
        P("pool", "context", None, None),
        P("pool", None),
        P("pool"),
        P("pool"),
        P("pool", "context", None),
        P("pool", "context", "tensor", None),
        P("pool", None, None),
        P(("context", "tensor"), None),
        P(),
        P("pool", None, "tensor", None),
    )
    return jax.shard_map(
        functools.partial(on_device, count=mesh.shape["context"]),
        mesh=mesh,
        in_specs=placed,
        out_specs=(
            P("pool", "context", "tensor", None),
            P("pool", None, "tensor", None),
            P("pool", None, None),
        ),
        check_vma=False,
    )
```

```python
import functools
import math

import jax
import jax.numpy as jnp
from jax import lax
from jax.experimental import pallas as pl
from jax.experimental.pallas import tpu as pltpu
from jax.sharding import PartitionSpec as P

SCALE = 192.0 ** (-0.5)
FACTOR = SCALE * 1.4426950408889634
NEG = -1e30
TILE = 16
LANES = 128
WIDE = 640
TAIL = 48
RADIX = 4
GROUPS = 16


def in_vmem(array):
    return pltpu.with_memory_space_constraint(array, pltpu.VMEM)


def in_hbm(array):
    return pltpu.with_memory_space_constraint(array, pltpu.HBM)


def dot(left, right):
    return jnp.dot(left, right, preferred_element_type=jnp.float32)


def score(keys, queries):
    return lax.dot_general(keys, queries, (((1,), (1,)), ((), ())), preferred_element_type=jnp.float32)


def pack_kernel(down_ref, hidden_ref, latent_ref, cache_ref, out_ref):
    core = lax.axis_index("tensor")
    down = down_ref[...]
    part, width = down.shape
    if hidden_ref.shape[1] == part:
        hidden = hidden_ref[...]
    else:
        pair = 2 * part
        start = pl.multiple_of(lax.axis_index("context") * pair, LANES)
        window = hidden_ref[:, pl.ds(start, pair)]
        hidden = jnp.where(core == 0, window[:, :part], window[:, part:])
    raw = dot(hidden, down)
    high = raw.astype(jnp.bfloat16).astype(jnp.float32)
    low = raw - high
    tok, cached = latent_ref.shape[1], cache_ref.shape[1]
    rows = tok + cached
    lat = width // LANES * LANES
    dec = raw.shape[0]
    for tile in range(2):
        at = pl.multiple_of(core * (lat // 2) + tile * LANES, LANES)
        out_ref[tile * rows : tile * rows + tok, :] = latent_ref[0, :, pl.ds(at, LANES)]
        out_ref[tile * rows + tok : (tile + 1) * rows, :] = cache_ref[0, :, pl.ds(at, LANES)]
    rope = jnp.concatenate(
        [latent_ref[0, :, lat:].astype(jnp.float32), cache_ref[0, :, lat:].astype(jnp.float32)], axis=0
    )
    left, right = split_rows(rows)
    rope = jnp.where(core == 0, rope[: rows // 2], rope[rows // 2 :])
    side = WIDE - width
    gap = jnp.zeros((left - right, side), jnp.float32)
    pieces = [jnp.concatenate([rope[:left], jnp.concatenate([rope[left:], gap], axis=0)], axis=1)]
    pieces += [piece[:, i : i + LANES] for piece in (high, low) for i in range(0, lat, LANES)]
    pieces.append(jnp.concatenate([high[:, lat:], low[:, lat:]], axis=1))
    used = sum(piece.shape[0] for piece in pieces)
    pieces.append(jnp.zeros((TAIL - used, LANES), jnp.float32))
    out_ref[2 * rows :, :] = jnp.concatenate(pieces, axis=0).astype(jnp.bfloat16)


def split_rows(rows):
    left = (rows // 4 + 7) // 8 * 8
    return left, rows // 2 - left


def stack_kernel(*refs):
    for i, ref in enumerate(refs[:-1]):
        refs[-1][i] = ref[...]


def fold(scores, values, state):
    top = jnp.max(scores, axis=0, keepdims=True)
    if state is not None:
        top = jnp.maximum(top, state[0])
    weights = jnp.exp2((scores - top) * FACTOR)
    whole = jnp.sum(weights, axis=0, keepdims=True)
    mixed = dot(values, weights.astype(jnp.bfloat16))
    if state is not None:
        fade = jnp.exp2((state[0] - top) * FACTOR)
        whole = whole + state[1] * fade
        mixed = mixed + state[2] * fade
    return top, whole, mixed


def ahead(order, begin, finish):
    started = begin(order[0])
    for block, following in zip(order, order[1:] + [None]):
        next_started = None if following is None else begin(following)
        finish(block, started)
        started = next_started


def read_state(mixed_ref, stat_ref, block, lanes, at=0):
    lanes = slice(at, at + lanes)
    return stat_ref[block, 0:1, lanes], stat_ref[block, 1:2, lanes], mixed_ref[block, :, lanes]


def write_state(mixed_ref, stat_ref, block, lanes, state):
    stat_ref[block, 0:1, :lanes] = state[0]
    stat_ref[block, 1:2, :lanes] = state[1]
    mixed_ref[block, :, :lanes] = state[2]


def table_kernel(shape, prefix_ref, length_ref, hits_hbm, gain_hbm, query_hbm, *refs):
    layout, tok, cached, block_rows = shape
    *table_refs, turn_ref, hot_ref, marked_ref, gain_ref, query_ref, hits_ref, sem, side_sem = refs
    steps, groups, heads, width = query_ref.shape

    def fetch(step):
        return pltpu.make_async_copy(
            query_hbm.at[0, pl.ds(step * groups, groups)], query_ref.at[step], sem.at[step]
        )

    fetch_hits = pltpu.make_async_copy(hits_hbm, hits_ref, side_sem.at[0])
    fetch_gain = pltpu.make_async_copy(gain_hbm, gain_ref, side_sem.at[1])
    fetch_hits.start()
    for step in range(steps):
        fetch(step).start()
    fetch_gain.start()
    token = lax.broadcasted_iota(jnp.int32, hot_ref.shape, 0)
    hot = token == lax.broadcasted_iota(jnp.int32, hot_ref.shape, 2)
    hot_ref[...] = jnp.where(hot, 1.0, 0.0).astype(jnp.bfloat16)
    fetch_hits.wait()
    me = lax.axis_index("context")
    prefix = prefix_ref[0]
    length = length_ref[0]
    slots = cached // block_rows
    first = LANES - tok

    lane = lax.broadcasted_iota(jnp.int32, (tok, LANES), 1)
    bound = jnp.where(lane < first, length - 1, me * tok + lane - first)
    token = lax.broadcasted_iota(jnp.int32, (tok, LANES), 0)
    for keys, table_ref in zip(layout, table_refs):
        for i, key in enumerate(keys):
            source = me ^ key
            at = i * (tok + cached)
            allowed = token + source * tok <= bound
            table_ref[at : at + tok] = jnp.where(allowed, 0.0, NEG).astype(jnp.bfloat16)
            for slot in range(slots):
                live = jnp.int32(0)
                for b in range(hits_ref.shape[1]):
                    hit = jnp.logical_and(hits_ref[0, b] == source * slots + slot, b < prefix)
                    live = jnp.where(hit, 1, live)
                spot = at + tok + slot * block_rows
                mask = jnp.where(jnp.full((block_rows, LANES), live, jnp.int32) == 1, 0.0, NEG)
                table_ref[spot : spot + block_rows] = mask.astype(jnp.bfloat16)

    dec, rope = turn_ref.shape[1:]
    half = rope // 2
    step = lax.broadcasted_iota(jnp.int32, (dec, rope), 0)
    lane = lax.broadcasted_iota(jnp.int32, (dec, rope), 1)
    number = jnp.where(lane < half, lane, lane - half).astype(jnp.float32)
    position = (prefix * block_rows + length + step).astype(jnp.float32)
    angle = position * jnp.exp2(number * (-math.log2(10000.0) / half))
    turn_ref[0] = jnp.cos(angle)
    sine = jnp.sin(angle)
    turn_ref[1] = jnp.where(lane < half, -sine, sine)

    rows = groups * heads
    for step in range(steps):
        fetch(step).wait()
        mark = hot_ref[step * groups : (step + 1) * groups].reshape(rows, WIDE - width)
        marked_ref[step] = jnp.concatenate([query_ref[step].reshape(rows, width), mark], axis=1)
    fetch_gain.wait()


def swap_halves(x):
    half = x.shape[1] // 2
    return jnp.concatenate([x[:, half:], x[:, :half]], axis=1)


def pick_block(marked_ref, late_ref, block):
    count = marked_ref.shape[0]
    return marked_ref[block] if block < count else late_ref[block - count]


def load_keys(keys_ref, pairs, table_ref, rows, side):
    core = lax.axis_index("tensor")
    left, right = split_rows(rows)
    in_key = lax.broadcasted_iota(jnp.int32, (rows, LANES), 1) < LANES - side
    at = 0
    for mine, theirs in pairs:
        halves = [jnp.where(core == 0, mine, theirs), jnp.where(core == 0, theirs, mine)]
        lane = 0
        tails = []
        for half in halves:
            for tile in range(2):
                keys_ref[at : at + rows, lane : lane + LANES] = half[tile * rows : (tile + 1) * rows]
                lane += LANES
            tail = half[2 * rows :].astype(jnp.float32)
            tails += [tail[:left], swap_halves(tail[:right])]
        rope = jnp.concatenate(tails, axis=0).astype(jnp.bfloat16)
        keys_ref[at : at + rows, lane:] = jnp.where(in_key, rope, table_ref[at : at + rows])
        at += rows


def middle_kernel(shape, marked_ref, late_ref, decode_ref, table_ref, *refs):
    counts, rows, side, order, blocks, loaded = shape
    kinds = len(counts)
    if loaded:
        mixed_ref, stat_ref = refs[2:]
        keys, values = refs[0][...], refs[1][...]
        before = ()
    else:
        mixed_ref, stat_ref, keys_ref, values_ref = refs[-4:]
        own, other = refs[:kinds], refs[kinds : 2 * kinds]
        before = refs[2 * kinds : -4]
        pairs = [(mine[i], theirs[i]) for mine, theirs, n in zip(own, other, counts) for i in range(n)]
        load_keys(keys_ref, pairs, table_ref, rows, side)
        keys = keys_ref[...]
        values_ref[...] = keys_ref[:, : values_ref.shape[0]].T
        values = values_ref[...]
    lanes_all = mixed_ref.shape[2]

    def lanes_of(index):
        return LANES if order[index] == blocks - 1 else lanes_all

    def begin(index):
        if order[index] == blocks - 1:
            return score(keys, decode_ref[...]) + table_ref[...].astype(jnp.float32)
        return score(keys, pick_block(marked_ref, late_ref, order[index]))

    def finish(index, scores):
        lanes = lanes_of(index)
        state = read_state(*before, index, lanes) if before else None
        write_state(mixed_ref, stat_ref, index, lanes, fold(scores, values, state))

    ahead(list(range(len(order))), begin, finish)


def last_kernel(
    shape, marked_ref, late_ref, decode_ref, table_ref, turn_ref, gain_ref, *refs
):
    counts, rows, heads, dec, width = shape
    kinds = len(counts)
    own, other = refs[:kinds], refs[kinds : 2 * kinds]
    states = [refs[2 * kinds : 2 * kinds + 2], refs[2 * kinds + 2 : 2 * kinds + 4]]
    out_hbm, decode_hbm, fresh_hbm = refs[2 * kinds + 4 : 2 * kinds + 7]
    keys_ref, out_ref, decode_out_ref, fresh_ref, sem = refs[2 * kinds + 7 :]
    cut, lat, lanes_all = states[0][0].shape
    blocks = cut + states[1][0].shape[0]
    steps = blocks - 1
    groups = lanes_all // heads
    side = WIDE - width

    def store(block, half):
        size = groups // 2
        return pltpu.make_async_copy(
            out_ref.at[block, pl.ds(half * size, size)],
            out_hbm.at[0, pl.ds(block * groups + half * size, size)],
            sem.at[block, half],
        )

    decode_store = pltpu.make_async_copy(decode_out_ref, decode_hbm, sem.at[steps, 0])
    fresh_store = pltpu.make_async_copy(fresh_ref, fresh_hbm, sem.at[steps, 1])

    pairs = [(own[-1][i], other[-1][i]) for i in range(counts[-1])]
    load_keys(keys_ref, pairs, table_ref, rows, side)
    values = keys_ref[:, :lat].T

    def fresh_keys():
        sums = None
        for ref, count in zip(own + other, counts + counts):
            for i in range(count):
                part = ref[i, 2 * rows :, :].astype(jnp.float32)
                sums = part if sums is None else sums + part
        at = split_rows(rows)[0]
        pieces = [sums[at + i * dec : at + (i + 1) * dec] for i in range(2 * lat // LANES + 1)]
        tiles = lat // LANES
        raw = [pieces[i] + pieces[tiles + i] for i in range(tiles)]
        rope = pieces[-1][:, :side] + pieces[-1][:, side:]
        latent = jnp.concatenate(raw, axis=1)
        mean = jnp.sum(latent * latent, axis=-1, keepdims=True) * (1.0 / lat)
        normed = latent * lax.rsqrt(mean + 1e-06) * gain_ref[...]
        rotated = rope * turn_ref[0] + swap_halves(rope) * turn_ref[1]
        fresh = jnp.concatenate([normed, rotated], axis=1)
        fresh_ref[0] = fresh.astype(jnp.bfloat16)
        fresh = jnp.concatenate([fresh, jnp.zeros((dec, side), jnp.float32)], axis=1)
        fresh = jnp.concatenate([fresh, jnp.zeros((TILE - dec, WIDE), jnp.float32)], axis=0)
        row = lax.broadcasted_iota(jnp.int32, (TILE, LANES), 0)
        lane = lax.broadcasted_iota(jnp.int32, (TILE, LANES), 1)
        shift = jnp.where(row <= lax.div(lane, heads), 0.0, NEG)
        return fresh.astype(jnp.bfloat16), jnp.where(row < dec, shift, NEG)

    fresh, fresh_shift = fresh_keys()
    fresh_store.start()

    def begin(block):
        if block == steps:
            return score(keys_ref[...], decode_ref[...]) + table_ref[...].astype(jnp.float32)
        return score(keys_ref[...], pick_block(marked_ref, late_ref, block))

    def finish(block, scores):
        half, index = (0, block) if block < cut else (1, block - cut)
        last = block == steps
        state = read_state(*states[half], index, LANES if last else lanes_all)
        state = fold(scores, values, state)
        if last:
            state = fold(score(fresh, decode_ref[...]) + fresh_shift, fresh[:, :lat].T, state)
        scale = 1.0 / state[1]
        if last:
            result = (state[2] * scale).astype(jnp.bfloat16).T
            decode_out_ref[0] = result[: dec * heads].reshape(dec, heads, lat)
            decode_store.start()
            return
        for half in range(2):
            some = slice(half * lanes_all // 2, (half + 1) * lanes_all // 2)
            result = (state[2][:, some] * scale[:, some]).astype(jnp.bfloat16).T
            out_ref[block, pl.ds(half * (groups // 2), groups // 2)] = result.reshape(-1, heads, lat)
            store(block, half).start()

    ahead([*range(steps - 1), steps, steps - 1], begin, finish)
    for block in range(steps):
        for half in range(2):
            store(block, half).wait()
    decode_store.wait()
    fresh_store.wait()


def on_device(
    cache,
    hit_slots,
    prefix_blocks,
    suffix_len,
    suffix_latent,
    suffix_query,
    decode_hidden,
    kv_down,
    kv_gain,
    decode_query,
    count,
):
    lat = kv_gain.shape[0]
    own_slots, block_rows, width = cache.shape[1:]
    cached = own_slots * block_rows
    tok = suffix_latent.shape[1]
    dec, heads = decode_query.shape[1:3]
    radix = math.gcd(count, RADIX)
    pages = count // radix
    vmem = pl.BlockSpec(memory_space=pltpu.VMEM)
    smem = pl.BlockSpec(memory_space=pltpu.SMEM)
    anywhere = pl.BlockSpec(memory_space=pl.ANY)
    small = pltpu.CompilerParams(vmem_limit_bytes=8 << 20)
    large = pltpu.CompilerParams(vmem_limit_bytes=24 << 20)

    part = kv_down.shape[0]
    hidden = decode_hidden[0]
    if 2 * part % LANES:
        part_index = lax.axis_index(("context", "tensor"))
        hidden = lax.dynamic_slice_in_dim(hidden, part_index * part, part, 1)
    block = tok + cached
    rows = 2 * block + TAIL
    message = pl.pallas_call(
        pack_kernel,
        out_shape=pltpu.VMEM((rows, LANES), jnp.bfloat16),
        in_specs=[vmem] * 4,
        out_specs=vmem,
        compiler_params=small,
    )(in_hbm(kv_down), in_hbm(hidden), in_hbm(suffix_latent), in_hbm(cache.reshape(1, cached, width)))

    def send(array, hop):
        return lax.ppermute(array, "context", [(rank, rank ^ hop) for rank in range(count)])

    def swap(array):
        return lax.ppermute(array, "tensor", [(0, 1), (1, 0)])

    def stack(*arrays, cost=None):
        return pl.pallas_call(
            stack_kernel,
            out_shape=pltpu.VMEM((len(arrays), rows, LANES), jnp.bfloat16),
            in_specs=[vmem] * len(arrays),
            out_specs=vmem,
            compiler_params=small,
            cost_estimate=cost,
        )(*arrays)

    hops = list(range(1, pages))
    leaps = [digit * pages for digit in range(1, radix)]
    layout = [[0, *hops, *leaps]] + [[leap + hop for leap in leaps] for hop in hops]
    beside = [send(message, hop) for hop in hops]
    across = [send(message, leap) for leap in leaps]

    groups = math.gcd(tok, GROUPS)
    steps = tok // groups
    lanes = groups * heads
    blocks = steps + 1

    first_steps = steps // 2
    *tables, turn, hot, marked, gain = pl.pallas_call(
        functools.partial(table_kernel, (layout, tok, cached, block_rows)),
        out_shape=tuple(pltpu.VMEM((len(keys) * block, LANES), jnp.bfloat16) for keys in layout)
        + (
            pltpu.VMEM((2, dec, width - lat), jnp.float32),
            pltpu.VMEM((tok, heads, WIDE - width), jnp.bfloat16),
            pltpu.VMEM((first_steps, lanes, WIDE), jnp.bfloat16),
            pltpu.VMEM((1, lat), jnp.float32),
        ),
        in_specs=[smem, smem, anywhere, anywhere, anywhere],
        out_specs=(vmem,) * (len(layout) + 4),
        scratch_shapes=[
            pltpu.VMEM((first_steps, groups, heads, width), jnp.bfloat16),
            pltpu.SMEM(hit_slots.shape, jnp.int32),
            pltpu.SemaphoreType.DMA((first_steps,)),
            pltpu.SemaphoreType.DMA((2,)),
        ],
        compiler_params=large,
    )(
        prefix_blocks,
        suffix_len,
        in_hbm(hit_slots),
        in_hbm(kv_gain.reshape(1, lat)),
        in_hbm(suffix_query),
    )

    def mark(query, begin, end):
        some = slice(begin * groups, end * groups)
        return jnp.concatenate([query[0, some], hot[some]], axis=2).reshape(end - begin, lanes, WIDE)

    held = lax.optimization_barrier((turn, hot, marked, *tables, *beside, *across))
    turn, hot, marked = held[:3]
    tables, held = held[3 : 3 + pages], held[3 + pages :]
    beside, across = held[: pages - 1], held[pages - 1 :]
    far = stack(*across)
    ends = [send(far, hop) for hop in hops]
    cost = pl.CostEstimate(flops=6 * 10**8, bytes_accessed=1 << 20, transcendentals=0)
    own = [stack(message, *beside, cost=cost), far]
    other = [swap(array) for array in own]
    later, far = lax.optimization_barrier((suffix_query, far))
    late = mark(later, first_steps, steps)

    def middle(decode_rows, table, own, other, order, *state, loaded=()):
        counts = [array.shape[0] for array in own]
        size = sum(counts) * block
        decode_rows = hot if decode_rows is None else decode_rows
        inputs = [in_vmem(marked), in_vmem(late), in_vmem(decode_rows), table]
        inputs += [*(loaded or (*own, *other)), *state]
        aliases = {len(inputs) - 2: 0, len(inputs) - 1: 1} if state else {}
        kept = () if loaded else ((size, WIDE), (lat, size))
        return pl.pallas_call(
            functools.partial(
                middle_kernel, (counts, block, WIDE - width, order, blocks, bool(loaded))
            ),
            out_shape=(
                pltpu.VMEM((len(order), lat, lanes), jnp.float32),
                pltpu.VMEM((len(order), 8, lanes), jnp.float32),
                *(pltpu.VMEM(shape, jnp.bfloat16) for shape in kept),
            ),
            in_specs=[vmem] * len(inputs),
            out_specs=(vmem,) * (2 + len(kept)),
            input_output_aliases=aliases,
            compiler_params=large,
        )(*inputs)

    orders = list(range(blocks - 2)), [blocks - 2, blocks - 1]
    mixed, stat, *loaded = middle(None, tables[0], own, other, orders[0])
    decode_rows, stat = lax.optimization_barrier((decode_query, stat))
    decode_rows = jnp.pad(
        decode_rows.reshape(dec * heads, width), ((0, LANES - dec * heads), (0, WIDE - width))
    )
    mixed, stat, decode_rows, *ends = lax.optimization_barrier((mixed, stat, decode_rows, *ends))
    states = [
        (mixed, stat),
        middle(decode_rows, tables[0], own, other, orders[1], loaded=loaded)[:2],
    ]
    own += ends
    other += [swap(array) for array in ends]
    for number in range(1, pages - 1):
        chosen = slice(1 + number, 2 + number)
        states = [
            middle(decode_rows, tables[number], own[chosen], other[chosen], order, *state)[:2]
            for order, state in zip(orders, states)
        ]
    counts = [array.shape[0] for array in own]
    return pl.pallas_call(
        functools.partial(last_kernel, (counts, block, heads, dec, width)),
        out_shape=(
            jax.ShapeDtypeStruct((1, tok, heads, lat), jnp.bfloat16),
            jax.ShapeDtypeStruct((1, dec, heads, lat), jnp.bfloat16),
            jax.ShapeDtypeStruct((1, dec, width), jnp.bfloat16),
        ),
        in_specs=[vmem] * (10 + 2 * len(own)),
        out_specs=(anywhere,) * 3,
        scratch_shapes=[
            pltpu.VMEM((counts[-1] * block, WIDE), jnp.bfloat16),
            pltpu.VMEM((steps, groups, heads, lat), jnp.bfloat16),
            pltpu.VMEM((1, dec, heads, lat), jnp.bfloat16),
            pltpu.VMEM((1, dec, width), jnp.bfloat16),
            pltpu.SemaphoreType.DMA((blocks, 2)),
        ],
        compiler_params=large,
    )(in_vmem(marked), in_vmem(late), in_vmem(decode_rows), tables[-1], turn, gain, *own, *other, *states[0], *states[1])


def solution(mesh):
    placed = (
        P("pool", "context", None, None),
        P("pool", None),
        P("pool"),
        P("pool"),
        P("pool", "context", None),
        P("pool", "context", "tensor", None),
        P("pool", None, None),
        P(("context", "tensor"), None),
        P(),
        P("pool", None, "tensor", None),
    )
    return jax.shard_map(
        functools.partial(on_device, count=mesh.shape["context"]),
        mesh=mesh,
        in_specs=placed,
        out_specs=(
            P("pool", "context", "tensor", None),
            P("pool", None, "tensor", None),
            P("pool", None, None),
        ),
        check_vma=False,
    )
```

```python
import functools
import math

import jax
import jax.numpy as jnp
from jax import lax
from jax.experimental import pallas as pl
from jax.experimental.pallas import tpu as pltpu
from jax.sharding import PartitionSpec as P

SCALE = 192.0 ** (-0.5)
FACTOR = SCALE * 1.4426950408889634
NEG = -1e30
TILE = 16
LANES = 128
WIDE = 640
TAIL = 48
RADIX = 4
GROUPS = 16


def in_vmem(array):
    return pltpu.with_memory_space_constraint(array, pltpu.VMEM)


def in_hbm(array):
    return pltpu.with_memory_space_constraint(array, pltpu.HBM)


def dot(left, right):
    return jnp.dot(left, right, preferred_element_type=jnp.float32)


def score(keys, queries):
    return lax.dot_general(keys, queries, (((1,), (1,)), ((), ())), preferred_element_type=jnp.float32)


def pack_kernel(down_ref, hidden_ref, latent_ref, cache_ref, out_ref):
    core = lax.axis_index("tensor")
    down = down_ref[...]
    part, width = down.shape
    if hidden_ref.shape[1] == part:
        hidden = hidden_ref[...]
    else:
        pair = 2 * part
        start = pl.multiple_of(lax.axis_index("context") * pair, LANES)
        window = hidden_ref[:, pl.ds(start, pair)]
        hidden = jnp.where(core == 0, window[:, :part], window[:, part:])
    raw = dot(hidden, down)
    high = raw.astype(jnp.bfloat16).astype(jnp.float32)
    low = raw - high
    tok, cached = latent_ref.shape[1], cache_ref.shape[1]
    rows = tok + cached
    lat = width // LANES * LANES
    dec = raw.shape[0]
    for tile in range(2):
        at = pl.multiple_of(core * (lat // 2) + tile * LANES, LANES)
        out_ref[tile * rows : tile * rows + tok, :] = latent_ref[0, :, pl.ds(at, LANES)]
        out_ref[tile * rows + tok : (tile + 1) * rows, :] = cache_ref[0, :, pl.ds(at, LANES)]
    rope = jnp.concatenate(
        [latent_ref[0, :, lat:].astype(jnp.float32), cache_ref[0, :, lat:].astype(jnp.float32)], axis=0
    )
    left, right = split_rows(rows)
    rope = jnp.where(core == 0, rope[: rows // 2], rope[rows // 2 :])
    side = WIDE - width
    gap = jnp.zeros((left - right, side), jnp.float32)
    pieces = [jnp.concatenate([rope[:left], jnp.concatenate([rope[left:], gap], axis=0)], axis=1)]
    pieces += [piece[:, i : i + LANES] for piece in (high, low) for i in range(0, lat, LANES)]
    pieces.append(jnp.concatenate([high[:, lat:], low[:, lat:]], axis=1))
    used = sum(piece.shape[0] for piece in pieces)
    pieces.append(jnp.zeros((TAIL - used, LANES), jnp.float32))
    out_ref[2 * rows :, :] = jnp.concatenate(pieces, axis=0).astype(jnp.bfloat16)


def split_rows(rows):
    left = (rows // 4 + 7) // 8 * 8
    return left, rows // 2 - left


def stack_kernel(*refs):
    for i, ref in enumerate(refs[:-1]):
        refs[-1][i] = ref[...]


def fold(scores, values, state):
    top = jnp.max(scores, axis=0, keepdims=True)
    if state is not None:
        top = jnp.maximum(top, state[0])
    weights = jnp.exp2((scores - top) * FACTOR)
    whole = jnp.sum(weights, axis=0, keepdims=True)
    mixed = dot(values, weights.astype(jnp.bfloat16))
    if state is not None:
        fade = jnp.exp2((state[0] - top) * FACTOR)
        whole = whole + state[1] * fade
        mixed = mixed + state[2] * fade
    return top, whole, mixed


def ahead(order, begin, finish):
    started = begin(order[0])
    for block, following in zip(order, order[1:] + [None]):
        next_started = None if following is None else begin(following)
        finish(block, started)
        started = next_started


def read_state(mixed_ref, stat_ref, block, lanes, at=0):
    lanes = slice(at, at + lanes)
    return stat_ref[block, 0:1, lanes], stat_ref[block, 1:2, lanes], mixed_ref[block, :, lanes]


def write_state(mixed_ref, stat_ref, block, lanes, state):
    stat_ref[block, 0:1, :lanes] = state[0]
    stat_ref[block, 1:2, :lanes] = state[1]
    mixed_ref[block, :, :lanes] = state[2]


def table_kernel(shape, prefix_ref, length_ref, hits_hbm, gain_hbm, query_hbm, *refs):
    layout, tok, cached, block_rows = shape
    *table_refs, turn_ref, hot_ref, marked_ref, gain_ref, query_ref, hits_ref, sem, side_sem = refs
    steps, groups, heads, width = query_ref.shape

    def fetch(step):
        return pltpu.make_async_copy(
            query_hbm.at[0, pl.ds(step * groups, groups)], query_ref.at[step], sem.at[step]
        )

    fetch_hits = pltpu.make_async_copy(hits_hbm, hits_ref, side_sem.at[0])
    fetch_gain = pltpu.make_async_copy(gain_hbm, gain_ref, side_sem.at[1])
    fetch_hits.start()
    for step in range(steps):
        fetch(step).start()
    fetch_gain.start()
    token = lax.broadcasted_iota(jnp.int32, hot_ref.shape, 0)
    hot = token == lax.broadcasted_iota(jnp.int32, hot_ref.shape, 2)
    hot_ref[...] = jnp.where(hot, 1.0, 0.0).astype(jnp.bfloat16)
    fetch_hits.wait()
    me = lax.axis_index("context")
    prefix = prefix_ref[0]
    length = length_ref[0]
    slots = cached // block_rows
    first = LANES - tok

    lane = lax.broadcasted_iota(jnp.int32, (tok, LANES), 1)
    bound = jnp.where(lane < first, length - 1, me * tok + lane - first)
    token = lax.broadcasted_iota(jnp.int32, (tok, LANES), 0)
    for keys, table_ref in zip(layout, table_refs):
        for i, key in enumerate(keys):
            source = me ^ key
            at = i * (tok + cached)
            allowed = token + source * tok <= bound
            table_ref[at : at + tok] = jnp.where(allowed, 0.0, NEG).astype(jnp.bfloat16)
            for slot in range(slots):
                live = jnp.int32(0)
                for b in range(hits_ref.shape[1]):
                    hit = jnp.logical_and(hits_ref[0, b] == source * slots + slot, b < prefix)
                    live = jnp.where(hit, 1, live)
                spot = at + tok + slot * block_rows
                mask = jnp.where(jnp.full((block_rows, LANES), live, jnp.int32) == 1, 0.0, NEG)
                table_ref[spot : spot + block_rows] = mask.astype(jnp.bfloat16)

    dec, rope = turn_ref.shape[1:]
    half = rope // 2
    step = lax.broadcasted_iota(jnp.int32, (dec, rope), 0)
    lane = lax.broadcasted_iota(jnp.int32, (dec, rope), 1)
    number = jnp.where(lane < half, lane, lane - half).astype(jnp.float32)
    position = (prefix * block_rows + length + step).astype(jnp.float32)
    angle = position * jnp.exp2(number * (-math.log2(10000.0) / half))
    turn_ref[0] = jnp.cos(angle)
    sine = jnp.sin(angle)
    turn_ref[1] = jnp.where(lane < half, -sine, sine)

    rows = groups * heads
    for step in range(steps):
        fetch(step).wait()
        mark = hot_ref[step * groups : (step + 1) * groups].reshape(rows, WIDE - width)
        marked_ref[step] = jnp.concatenate([query_ref[step].reshape(rows, width), mark], axis=1)
    fetch_gain.wait()


def swap_halves(x):
    half = x.shape[1] // 2
    return jnp.concatenate([x[:, half:], x[:, :half]], axis=1)


def pick_block(marked_ref, late_ref, block):
    count = marked_ref.shape[0]
    return marked_ref[block] if block < count else late_ref[block - count]


def load_keys(keys_ref, pairs, table_ref, rows, side):
    core = lax.axis_index("tensor")
    left, right = split_rows(rows)
    in_key = lax.broadcasted_iota(jnp.int32, (rows, LANES), 1) < LANES - side
    at = 0
    for mine, theirs in pairs:
        halves = [jnp.where(core == 0, mine, theirs), jnp.where(core == 0, theirs, mine)]
        lane = 0
        tails = []
        for half in halves:
            for tile in range(2):
                keys_ref[at : at + rows, lane : lane + LANES] = half[tile * rows : (tile + 1) * rows]
                lane += LANES
            tail = half[2 * rows :].astype(jnp.float32)
            tails += [tail[:left], swap_halves(tail[:right])]
        rope = jnp.concatenate(tails, axis=0).astype(jnp.bfloat16)
        keys_ref[at : at + rows, lane:] = jnp.where(in_key, rope, table_ref[at : at + rows])
        at += rows


def middle_kernel(shape, marked_ref, late_ref, decode_ref, table_ref, *refs):
    counts, rows, side, order, blocks, loaded = shape
    kinds = len(counts)
    if loaded:
        mixed_ref, stat_ref = refs[2:]
        keys, values = refs[0][...], refs[1][...]
        before = ()
    else:
        mixed_ref, stat_ref, keys_ref, values_ref = refs[-4:]
        own, other = refs[:kinds], refs[kinds : 2 * kinds]
        before = refs[2 * kinds : -4]
        pairs = [(mine[i], theirs[i]) for mine, theirs, n in zip(own, other, counts) for i in range(n)]
        load_keys(keys_ref, pairs, table_ref, rows, side)
        keys = keys_ref[...]
        values_ref[...] = keys_ref[:, : values_ref.shape[0]].T
        values = values_ref[...]
    lanes_all = mixed_ref.shape[2]

    def lanes_of(index):
        return LANES if order[index] == blocks - 1 else lanes_all

    def begin(index):
        if order[index] == blocks - 1:
            return score(keys, decode_ref[...]) + table_ref[...].astype(jnp.float32)
        return score(keys, pick_block(marked_ref, late_ref, order[index]))

    def finish(index, scores):
        lanes = lanes_of(index)
        state = read_state(*before, index, lanes) if before else None
        write_state(mixed_ref, stat_ref, index, lanes, fold(scores, values, state))

    ahead(list(range(len(order))), begin, finish)


def last_kernel(
    shape, marked_ref, late_ref, decode_ref, table_ref, turn_ref, gain_ref, *refs
):
    counts, rows, heads, dec, width = shape
    kinds = len(counts)
    own, other = refs[:kinds], refs[kinds : 2 * kinds]
    states = [refs[2 * kinds : 2 * kinds + 2], refs[2 * kinds + 2 : 2 * kinds + 4]]
    out_hbm, decode_hbm, fresh_hbm = refs[2 * kinds + 4 : 2 * kinds + 7]
    keys_ref, out_ref, decode_out_ref, fresh_ref, sem = refs[2 * kinds + 7 :]
    cut, lat, lanes_all = states[0][0].shape
    blocks = cut + states[1][0].shape[0]
    steps = blocks - 1
    groups = lanes_all // heads
    side = WIDE - width

    def store(block, half):
        size = groups // 2
        return pltpu.make_async_copy(
            out_ref.at[block, pl.ds(half * size, size)],
            out_hbm.at[0, pl.ds(block * groups + half * size, size)],
            sem.at[block, half],
        )

    decode_store = pltpu.make_async_copy(decode_out_ref, decode_hbm, sem.at[steps, 0])
    fresh_store = pltpu.make_async_copy(fresh_ref, fresh_hbm, sem.at[steps, 1])

    pairs = [(own[-1][i], other[-1][i]) for i in range(counts[-1])]
    load_keys(keys_ref, pairs, table_ref, rows, side)
    values = keys_ref[:, :lat].T

    def fresh_keys():
        sums = None
        for ref, count in zip(own + other, counts + counts):
            for i in range(count):
                part = ref[i, 2 * rows :, :].astype(jnp.float32)
                sums = part if sums is None else sums + part
        at = split_rows(rows)[0]
        pieces = [sums[at + i * dec : at + (i + 1) * dec] for i in range(2 * lat // LANES + 1)]
        tiles = lat // LANES
        raw = [pieces[i] + pieces[tiles + i] for i in range(tiles)]
        rope = pieces[-1][:, :side] + pieces[-1][:, side:]
        latent = jnp.concatenate(raw, axis=1)
        mean = jnp.sum(latent * latent, axis=-1, keepdims=True) * (1.0 / lat)
        normed = latent * lax.rsqrt(mean + 1e-06) * gain_ref[...]
        rotated = rope * turn_ref[0] + swap_halves(rope) * turn_ref[1]
        fresh = jnp.concatenate([normed, rotated], axis=1)
        fresh_ref[0] = fresh.astype(jnp.bfloat16)
        fresh = jnp.concatenate([fresh, jnp.zeros((dec, side), jnp.float32)], axis=1)
        fresh = jnp.concatenate([fresh, jnp.zeros((TILE - dec, WIDE), jnp.float32)], axis=0)
        row = lax.broadcasted_iota(jnp.int32, (TILE, LANES), 0)
        lane = lax.broadcasted_iota(jnp.int32, (TILE, LANES), 1)
        shift = jnp.where(row <= lax.div(lane, heads), 0.0, NEG)
        return fresh.astype(jnp.bfloat16), jnp.where(row < dec, shift, NEG)

    fresh, fresh_shift = fresh_keys()
    fresh_store.start()

    def begin(block):
        if block == steps:
            return score(keys_ref[...], decode_ref[...]) + table_ref[...].astype(jnp.float32)
        return score(keys_ref[...], pick_block(marked_ref, late_ref, block))

    def finish(block, scores):
        half, index = (0, block) if block < cut else (1, block - cut)
        last = block == steps
        state = read_state(*states[half], index, LANES if last else lanes_all)
        state = fold(scores, values, state)
        if last:
            state = fold(score(fresh, decode_ref[...]) + fresh_shift, fresh[:, :lat].T, state)
        scale = 1.0 / state[1]
        if last:
            result = (state[2] * scale).astype(jnp.bfloat16).T
            decode_out_ref[0] = result[: dec * heads].reshape(dec, heads, lat)
            decode_store.start()
            return
        for half in range(2):
            some = slice(half * lanes_all // 2, (half + 1) * lanes_all // 2)
            result = (state[2][:, some] * scale[:, some]).astype(jnp.bfloat16).T
            out_ref[block, pl.ds(half * (groups // 2), groups // 2)] = result.reshape(-1, heads, lat)
            store(block, half).start()

    ahead([*range(steps - 1), steps, steps - 1], begin, finish)
    for block in range(steps):
        for half in range(2):
            store(block, half).wait()
    decode_store.wait()
    fresh_store.wait()


def on_device(
    cache,
    hit_slots,
    prefix_blocks,
    suffix_len,
    suffix_latent,
    suffix_query,
    decode_hidden,
    kv_down,
    kv_gain,
    decode_query,
    count,
):
    lat = kv_gain.shape[0]
    own_slots, block_rows, width = cache.shape[1:]
    cached = own_slots * block_rows
    tok = suffix_latent.shape[1]
    dec, heads = decode_query.shape[1:3]
    radix = math.gcd(count, RADIX)
    pages = count // radix
    vmem = pl.BlockSpec(memory_space=pltpu.VMEM)
    smem = pl.BlockSpec(memory_space=pltpu.SMEM)
    anywhere = pl.BlockSpec(memory_space=pl.ANY)
    small = pltpu.CompilerParams(vmem_limit_bytes=8 << 20)
    large = pltpu.CompilerParams(vmem_limit_bytes=24 << 20)

    part = kv_down.shape[0]
    hidden = decode_hidden[0]
    if 2 * part % LANES:
        part_index = lax.axis_index(("context", "tensor"))
        hidden = lax.dynamic_slice_in_dim(hidden, part_index * part, part, 1)
    block = tok + cached
    rows = 2 * block + TAIL
    message = pl.pallas_call(
        pack_kernel,
        out_shape=pltpu.VMEM((rows, LANES), jnp.bfloat16),
        in_specs=[vmem] * 4,
        out_specs=vmem,
        compiler_params=small,
    )(in_hbm(kv_down), in_hbm(hidden), in_hbm(suffix_latent), in_hbm(cache.reshape(1, cached, width)))

    def send(array, hop):
        return lax.ppermute(array, "context", [(rank, rank ^ hop) for rank in range(count)])

    def swap(array):
        return lax.ppermute(array, "tensor", [(0, 1), (1, 0)])

    def stack(*arrays, cost=None):
        return pl.pallas_call(
            stack_kernel,
            out_shape=pltpu.VMEM((len(arrays), rows, LANES), jnp.bfloat16),
            in_specs=[vmem] * len(arrays),
            out_specs=vmem,
            compiler_params=small,
            cost_estimate=cost,
        )(*arrays)

    hops = list(range(1, pages))
    leaps = [digit * pages for digit in range(1, radix)]
    layout = [[0, *hops, *leaps]] + [[leap + hop for leap in leaps] for hop in hops]
    beside = [send(message, hop) for hop in hops]
    across = [send(message, leap) for leap in leaps]

    groups = math.gcd(tok, GROUPS)
    steps = tok // groups
    lanes = groups * heads
    blocks = steps + 1

    first_steps = steps - 1
    *tables, turn, hot, marked, gain = pl.pallas_call(
        functools.partial(table_kernel, (layout, tok, cached, block_rows)),
        out_shape=tuple(pltpu.VMEM((len(keys) * block, LANES), jnp.bfloat16) for keys in layout)
        + (
            pltpu.VMEM((2, dec, width - lat), jnp.float32),
            pltpu.VMEM((tok, heads, WIDE - width), jnp.bfloat16),
            pltpu.VMEM((first_steps, lanes, WIDE), jnp.bfloat16),
            pltpu.VMEM((1, lat), jnp.float32),
        ),
        in_specs=[smem, smem, anywhere, anywhere, anywhere],
        out_specs=(vmem,) * (len(layout) + 4),
        scratch_shapes=[
            pltpu.VMEM((first_steps, groups, heads, width), jnp.bfloat16),
            pltpu.SMEM(hit_slots.shape, jnp.int32),
            pltpu.SemaphoreType.DMA((first_steps,)),
            pltpu.SemaphoreType.DMA((2,)),
        ],
        compiler_params=large,
    )(
        prefix_blocks,
        suffix_len,
        in_hbm(hit_slots),
        in_hbm(kv_gain.reshape(1, lat)),
        in_hbm(suffix_query),
    )

    def mark(query, begin, end):
        some = slice(begin * groups, end * groups)
        return jnp.concatenate([query[0, some], hot[some]], axis=2).reshape(end - begin, lanes, WIDE)

    held = lax.optimization_barrier((turn, hot, marked, *tables, *beside, *across))
    turn, hot, marked = held[:3]
    tables, held = held[3 : 3 + pages], held[3 + pages :]
    beside, across = held[: pages - 1], held[pages - 1 :]
    far = stack(*across)
    ends = [send(far, hop) for hop in hops]
    cost = pl.CostEstimate(flops=6 * 10**8, bytes_accessed=1 << 20, transcendentals=0)
    own = [stack(message, *beside, cost=cost), far]
    other = [swap(array) for array in own]
    later, far = lax.optimization_barrier((suffix_query, far))
    late = mark(later, first_steps, steps)

    def middle(decode_rows, table, own, other, order, *state, loaded=()):
        counts = [array.shape[0] for array in own]
        size = sum(counts) * block
        decode_rows = hot if decode_rows is None else decode_rows
        inputs = [in_vmem(marked), in_vmem(late), in_vmem(decode_rows), table]
        inputs += [*(loaded or (*own, *other)), *state]
        aliases = {len(inputs) - 2: 0, len(inputs) - 1: 1} if state else {}
        kept = () if loaded else ((size, WIDE), (lat, size))
        return pl.pallas_call(
            functools.partial(
                middle_kernel, (counts, block, WIDE - width, order, blocks, bool(loaded))
            ),
            out_shape=(
                pltpu.VMEM((len(order), lat, lanes), jnp.float32),
                pltpu.VMEM((len(order), 8, lanes), jnp.float32),
                *(pltpu.VMEM(shape, jnp.bfloat16) for shape in kept),
            ),
            in_specs=[vmem] * len(inputs),
            out_specs=(vmem,) * (2 + len(kept)),
            input_output_aliases=aliases,
            compiler_params=large,
        )(*inputs)

    orders = list(range(blocks - 2)), [blocks - 2, blocks - 1]
    mixed, stat, *loaded = middle(None, tables[0], own, other, orders[0])
    decode_rows, stat = lax.optimization_barrier((decode_query, stat))
    decode_rows = jnp.pad(
        decode_rows.reshape(dec * heads, width), ((0, LANES - dec * heads), (0, WIDE - width))
    )
    mixed, stat, decode_rows, *ends = lax.optimization_barrier((mixed, stat, decode_rows, *ends))
    states = [
        (mixed, stat),
        middle(decode_rows, tables[0], own, other, orders[1], loaded=loaded)[:2],
    ]
    own += ends
    other += [swap(array) for array in ends]
    for number in range(1, pages - 1):
        chosen = slice(1 + number, 2 + number)
        states = [
            middle(decode_rows, tables[number], own[chosen], other[chosen], order, *state)[:2]
            for order, state in zip(orders, states)
        ]
    counts = [array.shape[0] for array in own]
    return pl.pallas_call(
        functools.partial(last_kernel, (counts, block, heads, dec, width)),
        out_shape=(
            jax.ShapeDtypeStruct((1, tok, heads, lat), jnp.bfloat16),
            jax.ShapeDtypeStruct((1, dec, heads, lat), jnp.bfloat16),
            jax.ShapeDtypeStruct((1, dec, width), jnp.bfloat16),
        ),
        in_specs=[vmem] * (10 + 2 * len(own)),
        out_specs=(anywhere,) * 3,
        scratch_shapes=[
            pltpu.VMEM((counts[-1] * block, WIDE), jnp.bfloat16),
            pltpu.VMEM((steps, groups, heads, lat), jnp.bfloat16),
            pltpu.VMEM((1, dec, heads, lat), jnp.bfloat16),
            pltpu.VMEM((1, dec, width), jnp.bfloat16),
            pltpu.SemaphoreType.DMA((blocks, 2)),
        ],
        compiler_params=large,
    )(in_vmem(marked), in_vmem(late), in_vmem(decode_rows), tables[-1], turn, gain, *own, *other, *states[0], *states[1])


def solution(mesh):
    placed = (
        P("pool", "context", None, None),
        P("pool", None),
        P("pool"),
        P("pool"),
        P("pool", "context", None),
        P("pool", "context", "tensor", None),
        P("pool", None, None),
        P(("context", "tensor"), None),
        P(),
        P("pool", None, "tensor", None),
    )
    return jax.shard_map(
        functools.partial(on_device, count=mesh.shape["context"]),
        mesh=mesh,
        in_specs=placed,
        out_specs=(
            P("pool", "context", "tensor", None),
            P("pool", None, "tensor", None),
            P("pool", None, None),
        ),
        check_vma=False,
    )
```
